512 devices in a mesh: rep: 64 (over y, z), ctx: 8 (over x, core).
Axes of the slice: x: 4, y: 8, z: 8, core: 2. Of those that a mesh axis runs over, the one named last changes fastest.
Arguments:
- cache_latent: bfloat16 [256, 96, 64, 512], P('rep', 'ctx'), may hold values from -6 to 6
- cache_rope: bfloat16 [256, 96, 4096], P('rep', 'ctx'), may hold values from -6 to 6
- lengths: int32 [256], P('rep'), may hold values from 64 to 6144, as said below
- move_slots: int32 [64, 2], P('rep'), may hold values from 0 to 3, as said below
- q_latent: bfloat16 [256, 2, 128, 512], P('rep'), may hold values from -8 to 8
- q_rope: bfloat16 [256, 2, 8192], P('rep'), may hold values from -8 to 8
- new_keys: bfloat16 [256, 2, 576], P('rep'), may hold values from -6 to 6
Outputs:
- attended: bfloat16 [256, 2, 128, 512], P('rep', None, 'ctx')
The draws below stay inside these ranges and needn't reach their ends.
Inputs may be any that keep to these rules, and one draw needn't show every extreme that they name: `lengths`: requests of replicas 64/2 and up hold 3072 or more tokens, the others 6144/2 or fewer; the last request holds exactly 6144. `move_slots`: each row lists 2 different slots.
All inputs are finite; a program needn't handle non-finite values.
Results may differ from the reference program's by a relative error of at most 0.005.
Values may be sent and summed in bfloat16 or wider, within the bound.
A program may use at most 64 MiB of HBM per device.

```python
import jax
import jax.numpy as jnp
from jax import lax

H = 128
LAT = 512
ROPE = 64
PAGE = 64
STEPS = 2
R_DEV = 4
PG_DEV = 12
MOVE = 2
REQUESTS = 256
CTX_PAGES = 96
LEN_MAX = 6144
N_REP = 64
N_CTX = 8


def draw_cache_latent(key, part):
    own_key = jax.random.fold_in(key, 11)
    shape = (REQUESTS, CTX_PAGES, PAGE, LAT)
    values = jnp.clip(jax.random.normal(own_key, shape, jnp.float32), -6.0, 6.0)
    return values.astype(jnp.bfloat16)


def draw_cache_rope(key, part):
    own_key = jax.random.fold_in(key, 12)
    shape = (REQUESTS, CTX_PAGES, PAGE * ROPE)
    values = jnp.clip(jax.random.normal(own_key, shape, jnp.float32), -6.0, 6.0)
    return values.astype(jnp.bfloat16)


def draw_q_latent(key, part):
    own_key = jax.random.fold_in(key, 13)
    shape = (REQUESTS, STEPS, H, LAT)
    values = jnp.clip(2.0 * jax.random.normal(own_key, shape, jnp.float32), -8.0, 8.0)
    return values.astype(jnp.bfloat16)


def draw_q_rope(key, part):
    own_key = jax.random.fold_in(key, 14)
    shape = (REQUESTS, STEPS, H, ROPE)
    values = jnp.clip(2.0 * jax.random.normal(own_key, shape, jnp.float32), -8.0, 8.0)
    return values.reshape(REQUESTS, STEPS, H * ROPE).astype(jnp.bfloat16)


def draw_lengths(key, part):
    key = jax.random.fold_in(key, 21)
    replica = jnp.arange(REQUESTS, dtype=jnp.int32) // R_DEV
    upper = replica >= N_REP // 2
    low = jax.random.randint(jax.random.fold_in(key, 1), (REQUESTS,), PAGE, LEN_MAX // 2 + 1)
    high = jax.random.randint(jax.random.fold_in(key, 2), (REQUESTS,), LEN_MAX // 2, LEN_MAX + 1)
    drawn = jnp.where(upper, high, low).astype(jnp.int32)
    return drawn.at[REQUESTS - 1].set(LEN_MAX)


def draw_move_slots(key, part):
    key = jax.random.fold_in(key, 31)
    scores = jax.random.randint(key, (N_REP, R_DEV), 0, 1 << 20) * R_DEV + jnp.arange(R_DEV, dtype=jnp.int32)[None, :]
    order = jnp.argsort(scores, axis=1, stable=True)
    return order[:, :MOVE].astype(jnp.int32)


def steps_of(key, dims, split, smallest, high):
    def one(dim, shards_of):
        heights = jax.random.uniform(jax.random.fold_in(jax.random.fold_in(key, 6), dim), (shards_of,), jnp.float32, smallest / len(split), high / len(split))
        return jnp.repeat(jnp.exp(heights), dims[dim] // shards_of).reshape((-1,) + (1,) * (len(dims) - dim - 1))

    gain = one(*split[0])
    for cut in split[1:]:
        gain = gain * one(*cut)
    return gain


def noise(rng, extent, scale, most, pieces=(), kind=jnp.bfloat16):
    factor_of = steps_of(rng, extent, pieces, -0.22, 0.18) if pieces else 1.0
    values = jax.random.normal(rng, extent, jnp.float32) * scale * factor_of
    return jnp.minimum(jnp.maximum(values, -most), most).astype(kind)


def setup_inputs(seed: int = 0) -> dict:
    key_list = jax.random.split(jax.random.key(seed), 8)
    cache_latent = draw_cache_latent(jax.random.fold_in(key_list[7], 71), 0)
    cache_rope = draw_cache_rope(jax.random.fold_in(key_list[7], 71), 0)
    lengths = draw_lengths(jax.random.fold_in(key_list[7], 71), 0)
    move_slots = draw_move_slots(jax.random.fold_in(key_list[7], 71), 0)
    q_latent = draw_q_latent(jax.random.fold_in(key_list[7], 71), 0)
    q_rope = draw_q_rope(jax.random.fold_in(key_list[7], 71), 0)
    new_keys = noise(key_list[6], (REQUESTS, STEPS, LAT + ROPE), 1.0, 6.0, ((0, 64),))
    return dict(cache_latent=cache_latent, cache_rope=cache_rope, lengths=lengths, move_slots=move_slots, q_latent=q_latent, q_rope=q_rope, new_keys=new_keys)


score_scale = 192.0 ** -0.5
masked = -1.0e30


def source_of(move_slots):
    replica = jnp.arange(N_REP, dtype=jnp.int32)
    partner = jnp.bitwise_xor(replica, N_REP // 2).astype(jnp.int32)
    own = replica[:, None] * R_DEV + jnp.arange(R_DEV, dtype=jnp.int32)[None, :]
    incoming = partner[:, None] * R_DEV + move_slots[partner]
    mapped = own.at[replica[:, None], move_slots].set(incoming.astype(jnp.int32))
    return mapped.reshape(-1).astype(jnp.int32)


def attend_one(item, cache_latent, cache_rope, lengths):
    source, q_lat, q_rot, fresh = item
    span = PG_DEV * PAGE
    keys = cache_latent[source].astype(jnp.float32).reshape(CTX_PAGES * PAGE, LAT)
    rot = cache_rope[source].astype(jnp.float32).reshape(CTX_PAGES * PAGE, ROPE)
    q_lat = q_lat.astype(jnp.float32)
    q_rot = q_rot.astype(jnp.float32).reshape(STEPS, H, ROPE)
    fresh = fresh.astype(jnp.float32)
    fresh_lat = fresh[:, :LAT]
    fresh_rot = fresh[:, LAT:]
    score = (jnp.einsum("shd,td->sht", q_lat, keys) + jnp.einsum("she,te->sht", q_rot, rot)) * score_scale
    new_score = (jnp.einsum("shd,nd->shn", q_lat, fresh_lat) + jnp.einsum("she,ne->shn", q_rot, fresh_rot)) * score_scale
    position = jnp.arange(CTX_PAGES * PAGE, dtype=jnp.int32)
    valid = (position < lengths[source]).reshape(1, 1, N_CTX, span)
    grouped = score.reshape(STEPS, H, N_CTX, span)
    step_ids = jnp.arange(STEPS, dtype=jnp.int32)
    new_valid = (step_ids[None, :] <= step_ids[:, None])[:, None, :]
    group_top = jnp.max(jnp.where(valid, grouped, masked), axis=-1)
    new_top = jnp.max(jnp.where(new_valid, new_score, masked), axis=-1)
    group_top = group_top.at[:, :, 0].set(jnp.maximum(group_top[:, :, 0], new_top))
    weights = jnp.where(valid, jnp.exp(grouped - group_top[..., None]), 0.0)
    new_weights = jnp.where(new_valid, jnp.exp(new_score - group_top[:, :, 0:1]), 0.0)
    totals = jnp.sum(weights, axis=-1)
    totals = totals.at[:, :, 0].add(jnp.sum(new_weights, axis=-1))
    rounded = lax.optimization_barrier(weights.astype(jnp.bfloat16)).astype(jnp.float32)
    new_rounded = lax.optimization_barrier(new_weights.astype(jnp.bfloat16)).astype(jnp.float32)
    values = keys.reshape(N_CTX, span, LAT)
    partial_value = jnp.einsum("shgt,gtd->shgd", rounded, values)
    partial_value = partial_value.at[:, :, 0].add(jnp.einsum("shn,nd->shd", new_rounded, fresh_lat))
    partial_value = lax.optimization_barrier(partial_value.astype(jnp.bfloat16)).astype(jnp.float32)
    overall = jnp.max(group_top, axis=-1)
    factor = jnp.exp(group_top - overall[..., None])
    numer = jnp.sum(factor[..., None] * partial_value, axis=2)
    denom = jnp.sum(factor * totals, axis=2)
    return (numer / denom[..., None]).astype(jnp.bfloat16)


def reference(cache_latent, cache_rope, lengths, move_slots, q_latent, q_rope, new_keys):
    source = source_of(move_slots)

    def one(item):
        return attend_one(item, cache_latent, cache_rope, lengths)

    return lax.map(one, (source, q_latent, q_rope, new_keys))
```

```python
import functools

import jax
import jax.numpy as jnp
import numpy as np
from jax import lax
from jax.experimental import pallas as pl
from jax.experimental.pallas import tpu as pltpu
from jax.sharding import PartitionSpec as P

score_scale = 192.0 ** (-0.5)
masked = -1e30
MESH = pl.DeviceIdType.MESH
F32 = jnp.float32
BF16 = jnp.bfloat16


def nt(a, b):
    return lax.dot_general(a, b, (((1,), (1,)), ((), ())), preferred_element_type=F32)


def nn(a, b):
    return lax.dot_general(a, b, (((1,), (0,)), ((), ())), preferred_element_type=F32)


def iota(shape, dim):
    return lax.broadcasted_iota(jnp.int32, shape, dim)


def spread_heads(pairs):
    n = pairs.shape[0]
    row, col = iota((2 * n, n), 0), iota((2 * n, n), 1)
    pick = jnp.where(col == (row >> 1), 1.0, 0.0).astype(BF16)
    both = nn(pick, pairs)
    row, lane = iota((2 * n, 128), 0), iota((2 * n, 128), 1)
    one = jnp.where((lane >> 6) == (row & 1), both, 0.0)
    return (one + pltpu.roll(one, 64, 1)).astype(BF16)


def stats_block(top, total):
    lane = iota((top.shape[0], 128), 1)
    block = jnp.zeros((top.shape[0], 128), F32)
    for at, value, terms in ((0, top, 3), (3, total, 2)):
        for n in range(terms):
            term = value.astype(BF16).astype(F32)
            block = jnp.where(lane == at + n, term, block)
            value = value - term
    return block.astype(BF16)


def read_stats(block):
    block = block.astype(F32)
    return block[:, 0:1] + block[:, 1:2] + block[:, 2:3], block[:, 3:4] + block[:, 4:5]


def kernel(
    n_rep,
    plan,
    lengths,
    moves,
    lat_hbm,
    rope_hbm,
    q_hbm,
    qr_hbm,
    nk_hbm,
    out,
    lat_v,
    rope_v,
    q_v,
    qown,
    qr_v,
    nk_v,
    xq,
    xk,
    rk,
    nkx,
    nkf,
    msg,
    qall,
    psend,
    precv,
    own,
    ownstat,
    rs,
    rr,
    newp,
    newstat,
    ysend,
    res,
    in_sem,
    y_s,
    y_r,
    ag_s,
    ag_r,
    sb_s,
    sb_r,
    p_s,
    p_r,
    r_s,
    r_r,
    o_s,
    o_r,
):
    rep = lax.axis_index("rep")
    ctx = lax.axis_index("ctx")
    cx = ctx // 2
    core = ctx % 2
    partner = {"rep": (rep + n_rep // 2) % n_rep, "ctx": ctx}
    sibling = {"rep": rep, "ctx": cx * 2 + (1 - core)}

    def chip(d):
        return {"rep": rep, "ctx": ((cx + d) % 4) * 2 + core}

    loads = {}

    def load(name, src, dst):
        copy = pltpu.make_async_copy(src, dst, in_sem.at[len(loads)])
        copy.start()
        loads[name] = copy

    for s in range(2):
        load(("own", s), q_hbm.at[:, s, pl.ds(pl.multiple_of(ctx * 16, 16), 16), :], qown.at[:, s])
    load("qr", qr_hbm, qr_v)
    load("nk", nk_hbm, nk_v)
    load("rope", rope_hbm, rope_v)
    for i in range(4):
        load(("lat", i), lat_hbm.at[i], lat_v.at[i])
    for g in range(8):
        c = (core + g // 4) % 2
        head = pl.multiple_of(((g % 4) * 2 + c) * 16, 16)
        for s in range(2):
            load(("q", g, s), q_hbm.at[:, s, pl.ds(head, 16), :], q_v.at[:, g, s])

    barrier = pltpu.get_barrier_semaphore()
    for peer in (partner, sibling, chip(1), chip(2), chip(3)):
        pl.semaphore_signal(barrier, inc=1, device_id=peer, device_id_type=MESH)

    row = (moves[0, 0] * 4 + moves[0, 1]) * 8
    slots = [plan[row + i] for i in range(4)]
    places = [plan[row + 4 + b] for b in range(4)]

    loads["qr"].wait()
    for i in range(4):
        rows = qr_v[i].astype(F32)
        for b in range(64):
            j = b // 8
            at = ((j % 2) * 4 + j // 2) * 16 + b % 8
            for s in range(2):
                xq[i, at + 8 * s : at + 8 * s + 1, :] = rows[s : s + 1, 128 * b : 128 * b + 128]

    def pairs_of(slot, c):
        return xq[slot, pl.ds(pl.multiple_of(c * 64, 64), 64), :].astype(BF16)

    def own_pairs(slot):
        return xq[slot, pl.ds(pl.multiple_of(core * 64 + cx * 16, 16), 16), :].astype(BF16)

    for name in (("own", 0), ("own", 1), "nk"):
        loads[name].wait()
    nkx[...] = jnp.zeros_like(nkx)
    for k in range(2):
        slot = slots[2 + k]
        msg[k, :, 0:512] = qown[slot].reshape(32, 512)
        msg[k, 0:16, 512:640] = own_pairs(slot)
        fresh = nk_v[slot].astype(F32)
        for n in range(2):
            for u in range(4):
                nkx[n * 4 + u : n * 4 + u + 1, :] = fresh[n : n + 1, 128 * u : 128 * u + 128]
            nkx[8 + n : 9 + n, 0:64] = fresh[n : n + 1, 512:576]
        msg[k, 16:32, 512:640] = nkx[...].astype(BF16)

    pl.semaphore_wait(barrier, 5)
    y_out = []
    for k in range(2):
        copy = pltpu.make_async_remote_copy(
            src_ref=msg.at[k],
            dst_ref=qall.at[k, cx],
            send_sem=y_s.at[k],
            recv_sem=y_r.at[k],
            device_id=partner,
            device_id_type=MESH,
        )
        copy.start()
        y_out.append(copy)

    loads["rope"].wait()
    xk[...] = jnp.zeros_like(xk)
    for i in range(4):
        for c in range(32):
            xk[c * 16 : c * 16 + 12, i * 128 : i * 128 + 128] = rope_v[i, :, c * 128 : c * 128 + 128]
    token, col = iota((768, 512), 0), iota((768, 512), 1)
    pick = jnp.where(col == ((token & 63) >> 1) * 16 + (token >> 6), 1.0, 0.0).astype(BF16)
    keys2 = nn(pick, xk[...])
    token, lane = iota((768, 128), 0), iota((768, 128), 1)
    keep = (lane >> 6) == (token & 1)
    for i in range(4):
        rk[i] = jnp.where(keep, keys2[:, i * 128 : i * 128 + 128], 0.0).astype(BF16)

    for i in range(4):
        loads[("lat", i)].wait()
    for g in range(8):
        for s in range(2):
            loads[("q", g, s)].wait()

    def attend(i, q, pairs):
        slot = slots[i]
        keys = lat_v[slot]
        score = (nt(q, keys) + nt(spread_heads(pairs), rk[slot])) * score_scale
        position = ctx * 768 + iota((1, 768), 1)
        valid = position < lengths[slot]
        score = jnp.where(valid, score, masked)
        top = jnp.max(score, axis=1, keepdims=True)
        weights = jnp.where(valid, jnp.exp(score - top), 0.0)
        total = jnp.sum(weights, axis=1, keepdims=True)
        part = nn(weights.astype(BF16), keys).astype(BF16)
        psend[i, :, 0:512] = part[128:256]
        psend[i, :, 512:640] = stats_block(top[128:256], total[128:256])
        copy = pltpu.make_async_remote_copy(
            src_ref=psend.at[i],
            dst_ref=precv.at[i],
            send_sem=p_s.at[i],
            recv_sem=p_r.at[i],
            device_id=sibling,
            device_id_type=MESH,
        )
        copy.start()
        own[i] = part[0:128]
        lane = iota((128, 128), 1)
        ownstat[i] = jnp.where(lane == 0, top[0:128], total[0:128])
        return copy

    def merge_cores(i, pair):
        pair.wait()
        top_a, total_a = ownstat[i, :, 0:1], ownstat[i, :, 1:2]
        top_b, total_b = read_stats(precv[i, :, 512:640])
        top = jnp.maximum(top_a, top_b)
        scale_a, scale_b = jnp.exp(top_a - top), jnp.exp(top_b - top)
        part = scale_a * own[i].astype(F32) + scale_b * precv[i, :, 0:512].astype(F32)
        rs[i, :, :, 0:512] = part.astype(BF16).reshape(4, 32, 512)
        stats = stats_block(top, scale_a * total_a + scale_b * total_b)
        rs[i, :, :, 512:640] = stats.reshape(4, 32, 128)
        copies = []
        for d in range(1, 4):
            copy = pltpu.make_async_remote_copy(
                src_ref=rs.at[i, (cx + d) % 4],
                dst_ref=rr.at[i, cx],
                send_sem=r_s.at[i, d],
                recv_sem=r_r.at[i, d],
                device_id=chip(d),
                device_id_type=MESH,
            )
            copy.start()
            copies.append(copy)
        rr[i, cx] = rs[i, cx]
        return copies

    def merge_chips(i, copies):
        for copy in copies:
            copy.wait()
        blocks = [rr[i, c] for c in range(4)]
        parts = [b[:, 0:512].astype(F32) for b in blocks] + [newp[i]]
        stats = [read_stats(b[:, 512:640]) for b in blocks]
        stats.append((newstat[i, :, 0:1], newstat[i, :, 1:2]))
        top = functools.reduce(jnp.maximum, [t for t, _ in stats])
        factors = [jnp.exp(t - top) for t, _ in stats]
        numer = sum(f * p for f, p in zip(factors, parts))
        denom = sum(f * t for f, (_, t) in zip(factors, stats))
        return (numer / denom).astype(BF16)

    pairs = [None] * 4
    chips = [None] * 4
    for i in range(2):
        slot = slots[i]
        both = jnp.concatenate([pairs_of(slot, core), pairs_of(slot, 1 - core)], axis=0)
        pairs[i] = attend(i, q_v[slot].reshape(256, 512), both)
    for i in range(2):
        chips[i] = merge_cores(i, pairs[i])

    gathers = []
    passes = []

    def to_sibling(k, d):
        c = (cx - d + 4) % 4
        copy = pltpu.make_async_remote_copy(
            src_ref=qall.at[k, c],
            dst_ref=qall.at[k, 4 + c],
            send_sem=sb_s.at[k, d],
            recv_sem=sb_r.at[k, d],
            device_id=sibling,
            device_id_type=MESH,
        )
        copy.start()
        passes.append((k, copy))

    for k in range(2):
        y_out[k].wait_recv()
        for d in (2, 1, 3):
            copy = pltpu.make_async_remote_copy(
                src_ref=qall.at[k, cx],
                dst_ref=qall.at[k, cx],
                send_sem=ag_s.at[k, d],
                recv_sem=ag_r.at[k, d],
                device_id=chip(d),
                device_id_type=MESH,
            )
            copy.start()
            gathers.append((k, d, copy))
        to_sibling(k, 0)

    nkf[...] = jnp.zeros_like(nkf)
    for i in range(2):
        nkf[2 * i : 2 * i + 2, 0:576] = nk_v[slots[i]].astype(F32)
    for k in range(2):
        fresh = qall[k, cx, 16:32, 512:640].astype(F32)
        for n in range(2):
            at = 4 + 2 * k + n
            for u in range(4):
                nkf[at : at + 1, 128 * u : 128 * u + 128] = fresh[n * 4 + u : n * 4 + u + 1, :]
            nkf[at : at + 1, 512:576] = fresh[8 + n : 9 + n, 0:64]
    fresh = nkf[...].astype(BF16)
    queries = [qown[slots[i]].reshape(32, 512) for i in range(2)] + [qall[k, cx, :, 0:512] for k in range(2)]
    queries = jnp.concatenate(queries, axis=0)
    rot = [own_pairs(slots[i]) for i in range(2)] + [qall[k, cx, 0:16, 512:640] for k in range(2)]
    rot = spread_heads(jnp.concatenate(rot, axis=0))
    score = (nt(queries, fresh[:, 0:512]) + nt(rot, fresh[:, 512:640])) * score_scale
    row, col = iota((128, 128), 0), iota((128, 128), 1)
    valid = ((row >> 5) == (col >> 1)) & ((col & 1) <= ((row >> 4) & 1))
    score = jnp.where(valid, score, masked)
    top = jnp.max(score, axis=1, keepdims=True)
    weights = jnp.where(valid, jnp.exp(score - top), 0.0)
    total = jnp.sum(weights, axis=1, keepdims=True)
    newp[...] = nn(weights.astype(BF16), fresh[:, 0:512]).reshape(4, 32, 512)
    newstat[...] = jnp.where(col == 0, top, total).reshape(4, 32, 128)

    for k, d, copy in gathers:
        copy.wait_recv()
        to_sibling(k, d)

    for k in range(2):
        for kk, copy in passes:
            if kk == k:
                copy.wait_recv()
        rot = qall[k, :, 0:16, 512:640].reshape(128, 128)
        pairs[2 + k] = attend(2 + k, qall[k, :, :, 0:512].reshape(256, 512), rot)
    for k in range(2):
        chips[2 + k] = merge_cores(2 + k, pairs[2 + k])

    for i in range(2):
        res[i] = merge_chips(i, chips[i])
    home = []
    for k in range(2):
        ysend[k] = merge_chips(2 + k, chips[2 + k])
        copy = pltpu.make_async_remote_copy(
            src_ref=ysend.at[k],
            dst_ref=res.at[2 + k],
            send_sem=o_s.at[k],
            recv_sem=o_r.at[k],
            device_id=partner,
            device_id_type=MESH,
        )
        copy.start()
        home.append(copy)

    for copy in y_out:
        copy.wait_send()
    for _, _, copy in gathers:
        copy.wait_send()
    for _, copy in passes:
        copy.wait_send()
    for copy in home:
        copy.wait()

    for b in range(4):
        out[b] = res[places[b]]


def plan_table():
    rows = np.zeros((4, 4, 8), np.int32)
    for first in range(4):
        for second in range(4):
            stay = [b for b in range(4) if b not in (first, second)]
            slots = (stay + [first, second])[:4] if first != second else [0, 1, 2, 3]
            rows[first, second, :4] = slots
            rows[first, second, 4:] = [slots.index(b) for b in range(4)]
    return rows.reshape(128)


def body(cache_latent, cache_rope, lengths, move_slots, q_latent, q_rope, new_keys):
    dma = pltpu.SemaphoreType.DMA
    smem = pl.BlockSpec(memory_space=pltpu.SMEM)
    hbm = pl.BlockSpec(memory_space=pl.ANY)
    out = pl.pallas_call(
        functools.partial(kernel, lax.axis_size("rep")),
        out_shape=jax.ShapeDtypeStruct((4, 32, 512), BF16),
        in_specs=[smem, smem, smem, hbm, hbm, hbm, hbm, hbm],
        out_specs=pl.BlockSpec(memory_space=pltpu.VMEM),
        scratch_shapes=[
            pltpu.VMEM((4, 768, 512), BF16),
            pltpu.VMEM((4, 12, 4096), BF16),
            pltpu.VMEM((4, 8, 2, 16, 512), BF16),
            pltpu.VMEM((4, 2, 16, 512), BF16),
            pltpu.VMEM((4, 2, 8192), BF16),
            pltpu.VMEM((4, 2, 576), BF16),
            pltpu.VMEM((4, 128, 128), F32),
            pltpu.VMEM((512, 512), BF16),
            pltpu.VMEM((4, 768, 128), BF16),
            pltpu.VMEM((16, 128), F32),
            pltpu.VMEM((128, 640), F32),
            pltpu.VMEM((2, 32, 640), BF16),
            pltpu.VMEM((2, 8, 32, 640), BF16),
            pltpu.VMEM((4, 128, 640), BF16),
            pltpu.VMEM((4, 128, 640), BF16),
            pltpu.VMEM((4, 128, 512), BF16),
            pltpu.VMEM((4, 128, 128), F32),
            pltpu.VMEM((4, 4, 32, 640), BF16),
            pltpu.VMEM((4, 4, 32, 640), BF16),
            pltpu.VMEM((4, 32, 512), F32),
            pltpu.VMEM((4, 32, 128), F32),
            pltpu.VMEM((2, 32, 512), BF16),
            pltpu.VMEM((4, 32, 512), BF16),
            dma((32,)),
            dma((2,)),
            dma((2,)),
            dma((2, 4)),
            dma((2, 4)),
            dma((2, 4)),
            dma((2, 4)),
            dma((4,)),
            dma((4,)),
            dma((4, 4)),
            dma((4, 4)),
            dma((2,)),
            dma((2,)),
        ],
        compiler_params=pltpu.CompilerParams(
            collective_id=0, has_side_effects=True, vmem_limit_bytes=48 * 1024 * 1024
        ),
        cost_estimate=pl.CostEstimate(flops=1800000000, bytes_accessed=4800000, transcendentals=800000),
    )(
        jnp.asarray(plan_table()),
        lengths,
        move_slots,
        cache_latent.reshape(4, 768, 512),
        cache_rope,
        q_latent,
        q_rope,
        new_keys,
    )
    return out.reshape(4, 2, 16, 512)


def solution(mesh):
    in_specs = (
        P("rep", "ctx", None, None),
        P("rep", "ctx", None),
        P("rep"),
        P("rep", None),
        P("rep", None, None, None),
        P("rep", None, None),
        P("rep", None, None),
    )
    out_specs = P("rep", None, "ctx", None)
    return jax.shard_map(body, mesh=mesh, in_specs=in_specs, out_specs=out_specs, check_vma=False)
```

```python
import functools

import jax
import jax.numpy as jnp
import numpy as np
from jax import lax
from jax.experimental import pallas as pl
from jax.experimental.pallas import tpu as pltpu
from jax.sharding import PartitionSpec as P

score_scale = 192.0 ** (-0.5)
masked = -1e30
MESH = pl.DeviceIdType.MESH
F32 = jnp.float32
BF16 = jnp.bfloat16


def nt(a, b):
    return lax.dot_general(a, b, (((1,), (1,)), ((), ())), preferred_element_type=F32)


def nn(a, b):
    return lax.dot_general(a, b, (((1,), (0,)), ((), ())), preferred_element_type=F32)


def iota(shape, dim):
    return lax.broadcasted_iota(jnp.int32, shape, dim)


def spread_heads(pairs):
    n = pairs.shape[0]
    row, col = iota((2 * n, n), 0), iota((2 * n, n), 1)
    pick = jnp.where(col == (row >> 1), 1.0, 0.0).astype(BF16)
    both = nn(pick, pairs)
    row, lane = iota((2 * n, 128), 0), iota((2 * n, 128), 1)
    one = jnp.where((lane >> 6) == (row & 1), both, 0.0)
    return (one + pltpu.roll(one, 64, 1)).astype(BF16)


def stats_block(top, total):
    lane = iota((top.shape[0], 128), 1)
    block = jnp.zeros((top.shape[0], 128), F32)
    for at, value, terms in ((0, top, 3), (3, total, 2)):
        for n in range(terms):
            term = value.astype(BF16).astype(F32)
            block = jnp.where(lane == at + n, term, block)
            value = value - term
    return block.astype(BF16)


def read_stats(block):
    block = block.astype(F32)
    return block[:, 0:1] + block[:, 1:2] + block[:, 2:3], block[:, 3:4] + block[:, 4:5]


def kernel(
    n_rep,
    tab_hbm,
    len_hbm,
    mov_hbm,
    lat_hbm,
    rope_hbm,
    q_hbm,
    qr_hbm,
    nk_hbm,
    out,
    keys,
    rope_v,
    q_v,
    qown,
    qr_v,
    nk_v,
    xq,
    xk,
    nkx,
    nkf,
    msg,
    nkmsg,
    nkgot,
    qall,
    pages,
    got,
    psend,
    precv,
    own,
    ownstat,
    rs,
    rr,
    newp,
    newstat,
    ysend,
    res,
    tab_s,
    len_s,
    mov_s,
    in_sem,
    y_s,
    y_r,
    ag_s,
    ag_r,
    k_s,
    k_r,
    p_s,
    p_r,
    r_s,
    r_r,
    o_s,
    o_r,
):
    rep = lax.axis_index("rep")
    ctx = lax.axis_index("ctx")
    cx = ctx // 2
    core = ctx % 2
    partner = {"rep": (rep + n_rep // 2) % n_rep, "ctx": ctx}
    other = cx * 2 + (1 - core)
    sibling = {"rep": rep, "ctx": other}

    def chip(d):
        return {"rep": rep, "ctx": ((cx + d) % 4) * 2 + core}

    barrier = pltpu.get_barrier_semaphore()
    for peer in (partner, chip(2), chip(1), chip(3), sibling):
        pl.semaphore_signal(barrier, inc=1, device_id=peer, device_id_type=MESH)

    loads = {}

    def load(name, src, dst):
        copy = pltpu.make_async_copy(src, dst, in_sem.at[len(loads)])
        copy.start()
        loads[name] = copy

    load("plan", tab_hbm, tab_s)
    load("moves", mov_hbm, mov_s)
    load("lengths", len_hbm, len_s)
    load("qr", qr_hbm, qr_v)
    for s in range(2):
        load(("own", s), q_hbm.at[:, s, pl.ds(pl.multiple_of(ctx * 16, 16), 16), :], qown.at[:, s])
    load("nk", nk_hbm, nk_v)
    load("rope", rope_hbm, rope_v)
    for i in range(4):
        load(("lat", i), lat_hbm.at[i], keys.at[i, :, 0:512])
    for g in range(8):
        c = (core + g // 4) % 2
        head = pl.multiple_of(((g % 4) * 2 + c) * 16, 16)
        for s in range(2):
            load(("q", g, s), q_hbm.at[:, s, pl.ds(head, 16), :], q_v.at[:, g, s])

    def remote(src, dst, send_sem, recv_sem, device):
        copy = pltpu.make_async_remote_copy(
            src_ref=src,
            dst_ref=dst,
            send_sem=send_sem,
            recv_sem=recv_sem,
            device_id=device,
            device_id_type=MESH,
        )
        copy.start()
        return copy

    loads["qr"].wait()
    for i in range(4):
        rows = qr_v[i].astype(F32)
        for b in range(64):
            j = b // 8
            at = ((j % 2) * 4 + j // 2) * 16 + b % 8
            for s in range(2):
                xq[i, at + 8 * s : at + 8 * s + 1, :] = rows[s : s + 1, 128 * b : 128 * b + 128]

    for name in ("plan", "lengths", "moves"):
        loads[name].wait()
    row = (mov_s[0, 0] * 4 + mov_s[0, 1]) * 8
    slots = [tab_s[row + i] for i in range(4)]
    places = [tab_s[row + 4 + b] for b in range(4)]

    def pairs_of(slot, c):
        return xq[slot, pl.ds(pl.multiple_of(c * 64, 64), 64), :].astype(BF16)

    def own_pairs(slot):
        return xq[slot, pl.ds(pl.multiple_of(core * 64 + cx * 16, 16), 16), :].astype(BF16)

    for name in (("own", 0), ("own", 1), "nk"):
        loads[name].wait()
    nkx[...] = jnp.zeros_like(nkx)
    for k in range(2):
        slot = slots[2 + k]
        msg[k, :, 0:512] = qown[slot].reshape(32, 512)
        msg[k, :, 512:640] = spread_heads(own_pairs(slot))
        fresh = nk_v[slot].astype(F32)
        for n in range(2):
            for u in range(4):
                nkx[n * 4 + u : n * 4 + u + 1, :] = fresh[n : n + 1, 128 * u : 128 * u + 128]
            nkx[8 + n : 9 + n, 0:64] = fresh[n : n + 1, 512:576]
        nkmsg[k] = nkx[...].astype(BF16)

    def rope_keys():
        loads["rope"].wait()
        for page in range(12):
            rows = rope_v[page].astype(F32)
            for c in range(32):
                for i in range(4):
                    at = page * 32 + c
                    xk[i, at : at + 1, :] = rows[i : i + 1, c * 128 : c * 128 + 128]
        token, col = iota((768, 384), 0), iota((768, 384), 1)
        pick = jnp.where(col == (token >> 1), 1.0, 0.0).astype(BF16)
        token, lane = iota((768, 128), 0), iota((768, 128), 1)
        keep = (lane >> 6) == (token & 1)
        both = nn(pick, jnp.concatenate([xk[i].astype(BF16) for i in range(4)], axis=1))
        for i in range(4):
            keys[i, :, 512:640] = jnp.where(keep, both[:, i * 128 : i * 128 + 128], 0.0).astype(BF16)
        for i in range(4):
            loads[("lat", i)].wait()
        for k in range(2):
            pages[k] = keys[slots[2 + k]]

    def attend(q, held, group, length):
        score = nt(q, held) * score_scale
        valid = group * 768 + iota((1, 768), 1) < length
        score = jnp.where(valid, score, masked)
        top = jnp.max(score, axis=1, keepdims=True)
        weights = jnp.where(valid, jnp.exp(score - top), 0.0)
        total = jnp.sum(weights, axis=1, keepdims=True)
        return nn(weights.astype(BF16), held[:, 0:512]).astype(BF16), top, total

    def stay(i):
        slot = slots[i]
        pairs = jnp.concatenate([pairs_of(slot, core), pairs_of(slot, 1 - core)], axis=0)
        q = jnp.concatenate([q_v[slot].reshape(256, 512), spread_heads(pairs)], axis=1)
        part, top, total = attend(q, keys[slot], ctx, len_s[slot])
        psend[i, :, 0:512] = part[128:256]
        psend[i, :, 512:640] = stats_block(top[128:256], total[128:256])
        own[i] = part[0:128]
        lane = iota((128, 128), 1)
        ownstat[i] = jnp.where(lane == 0, top[0:128], total[0:128])

    def merge(i, a, b):
        part_a, top_a, total_a = a
        part_b, top_b, total_b = b
        top = jnp.maximum(top_a, top_b)
        scale_a, scale_b = jnp.exp(top_a - top), jnp.exp(top_b - top)
        part = scale_a * part_a.astype(F32) + scale_b * part_b.astype(F32)
        rs[i, :, :, 0:512] = part.astype(BF16).reshape(4, 32, 512)
        stats = stats_block(top, scale_a * total_a + scale_b * total_b)
        rs[i, :, :, 512:640] = stats.reshape(4, 32, 128)
        copies = []
        for d in (2, 1, 3):
            src = rs.at[i, (cx + d) % 4]
            copies.append(remote(src, rr.at[i, cx], r_s.at[i, d], r_r.at[i, d], chip(d)))
        rr[i, cx] = rs[i, cx]
        return copies

    def merge_cores(i):
        pairs[i].wait()
        top, total = read_stats(precv[i, :, 512:640])
        return merge(
            i,
            (own[i], ownstat[i, :, 0:1], ownstat[i, :, 1:2]),
            (precv[i, :, 0:512], top, total),
        )

    def merge_chips(i):
        for copy in chips[i]:
            copy.wait()
        blocks = [rr[i, c] for c in range(4)]
        parts = [b[:, 0:512].astype(F32) for b in blocks] + [newp[i]]
        stats = [read_stats(b[:, 512:640]) for b in blocks]
        stats.append((newstat[i, :, 0:1], newstat[i, :, 1:2]))
        top = functools.reduce(jnp.maximum, [t for t, _ in stats])
        factors = [jnp.exp(t - top) for t, _ in stats]
        numer = sum(f * p for f, p in zip(factors, parts))
        denom = sum(f * t for f, (_, t) in zip(factors, stats))
        return (numer / denom).astype(BF16)

    def new_tokens():
        nkf[...] = jnp.zeros_like(nkf)
        for i in range(2):
            nkf[2 * i : 2 * i + 2, 0:576] = nk_v[slots[i]].astype(F32)
        for k in range(2):
            fresh = nkgot[k].astype(F32)
            for n in range(2):
                at = 4 + 2 * k + n
                for u in range(4):
                    nkf[at : at + 1, 128 * u : 128 * u + 128] = fresh[n * 4 + u : n * 4 + u + 1, :]
                nkf[at : at + 1, 512:576] = fresh[8 + n : 9 + n, 0:64]
        fresh = nkf[...].astype(BF16)
        queries = [
            jnp.concatenate([qown[slots[i]].reshape(32, 512), spread_heads(own_pairs(slots[i]))], axis=1)
            for i in range(2)
        ]
        queries = jnp.concatenate(queries + [qall[k, cx] for k in range(2)], axis=0)
        score = nt(queries, fresh) * score_scale
        row, col = iota((128, 128), 0), iota((128, 128), 1)
        valid = ((row >> 5) == (col >> 1)) & ((col & 1) <= ((row >> 4) & 1))
        score = jnp.where(valid, score, masked)
        top = jnp.max(score, axis=1, keepdims=True)
        weights = jnp.where(valid, jnp.exp(score - top), 0.0)
        total = jnp.sum(weights, axis=1, keepdims=True)
        newp[...] = nn(weights.astype(BF16), fresh[:, 0:512]).reshape(4, 32, 512)
        newstat[...] = jnp.where(col == 0, top, total).reshape(4, 32, 128)

    pairs = [None] * 2
    chips = [None] * 4

    rope_keys()
    for g in range(8):
        for s in range(2):
            loads[("q", g, s)].wait()

    pl.semaphore_wait(barrier, 5)
    y_out = [remote(msg.at[k], qall.at[k, cx], y_s.at[k], y_r.at[k], partner) for k in range(2)]
    y_out.append(remote(nkmsg, nkgot, y_s.at[2], y_r.at[2], partner))
    page_out = [remote(pages.at[k], got.at[k], k_s.at[k], k_r.at[k], sibling) for k in range(2)]
    for i in range(2):
        stay(i)
        pairs[i] = remote(psend.at[i], precv.at[i], p_s.at[i], p_r.at[i], sibling)

    gathers = []
    for k in range(2):
        y_out[k].wait_recv()
        for d in (2, 1, 3):
            gathers.append(remote(qall.at[k, cx], qall.at[k, cx], ag_s.at[k, d], ag_r.at[k, d], chip(d)))
    y_out[2].wait_recv()
    new_tokens()

    for k in range(2):
        i, length = 2 + k, len_s[slots[2 + k]]
        page_out[k].wait_recv()
        for copy in gathers[3 * k : 3 * k + 3]:
            copy.wait_recv()
        q = qall[k].reshape(128, 640)
        chips[i] = merge(i, attend(q, pages[k], ctx, length), attend(q, got[k], other, length))
    chips[0] = merge_cores(0)
    chips[1] = merge_cores(1)

    home = []
    for k in range(2):
        ysend[k] = merge_chips(2 + k)
        home.append(remote(ysend.at[k], res.at[2 + k], o_s.at[k], o_r.at[k], partner))
    for i in range(2):
        res[i] = merge_chips(i)

    for copy in y_out + page_out + gathers:
        copy.wait_send()
    for copy in home:
        copy.wait()

    for b in range(4):
        out[b] = res[places[b]]


def plan_table():
    rows = np.zeros((4, 4, 8), np.int32)
    for first in range(4):
        for second in range(4):
            stay = [b for b in range(4) if b not in (first, second)]
            slots = (stay + [first, second])[:4] if first != second else [0, 1, 2, 3]
            rows[first, second, :4] = slots
            rows[first, second, 4:] = [slots.index(b) for b in range(4)]
    return rows.reshape(128)


def body(cache_latent, cache_rope, lengths, move_slots, q_latent, q_rope, new_keys):
    dma = pltpu.SemaphoreType.DMA
    hbm = pl.BlockSpec(memory_space=pltpu.HBM)
    out = pl.pallas_call(
        functools.partial(kernel, lax.axis_size("rep")),
        out_shape=jax.ShapeDtypeStruct((4, 32, 512), BF16),
        in_specs=[hbm] * 8,
        out_specs=pl.BlockSpec(memory_space=pltpu.VMEM),
        scratch_shapes=[
            pltpu.VMEM((4, 768, 640), BF16),
            pltpu.VMEM((12, 4, 4096), BF16),
            pltpu.VMEM((4, 8, 2, 16, 512), BF16),
            pltpu.VMEM((4, 2, 16, 512), BF16),
            pltpu.VMEM((4, 2, 8192), BF16),
            pltpu.VMEM((4, 2, 576), BF16),
            pltpu.VMEM((4, 128, 128), F32),
            pltpu.VMEM((4, 384, 128), F32),
            pltpu.VMEM((16, 128), F32),
            pltpu.VMEM((128, 640), F32),
            pltpu.VMEM((2, 32, 640), BF16),
            pltpu.VMEM((2, 16, 128), BF16),
            pltpu.VMEM((2, 16, 128), BF16),
            pltpu.VMEM((2, 4, 32, 640), BF16),
            pltpu.VMEM((2, 768, 640), BF16),
            pltpu.VMEM((2, 768, 640), BF16),
            pltpu.VMEM((2, 128, 640), BF16),
            pltpu.VMEM((2, 128, 640), BF16),
            pltpu.VMEM((2, 128, 512), BF16),
            pltpu.VMEM((2, 128, 128), F32),
            pltpu.VMEM((4, 4, 32, 640), BF16),
            pltpu.VMEM((4, 4, 32, 640), BF16),
            pltpu.VMEM((4, 32, 512), F32),
            pltpu.VMEM((4, 32, 128), F32),
            pltpu.VMEM((2, 32, 512), BF16),
            pltpu.VMEM((4, 32, 512), BF16),
            pltpu.SMEM((128,), jnp.int32),
            pltpu.SMEM((4,), jnp.int32),
            pltpu.SMEM((1, 2), jnp.int32),
            dma((32,)),
            dma((3,)),
            dma((3,)),
            dma((2, 4)),
            dma((2, 4)),
            dma((2,)),
            dma((2,)),
            dma((2,)),
            dma((2,)),
            dma((4, 4)),
            dma((4, 4)),
            dma((2,)),
            dma((2,)),
        ],
        compiler_params=pltpu.CompilerParams(
            collective_id=0, has_side_effects=True, vmem_limit_bytes=66000000
        ),
        cost_estimate=pl.CostEstimate(flops=1800000000, bytes_accessed=4800000, transcendentals=800000),
    )(
        jnp.asarray(plan_table()),
        lengths,
        move_slots,
        cache_latent.reshape(4, 768, 512),
        cache_rope.transpose(1, 0, 2),
        q_latent,
        q_rope,
        new_keys,
    )
    return out.reshape(4, 2, 16, 512)


def solution(mesh):
    in_specs = (
        P("rep", "ctx", None, None),
        P("rep", "ctx", None),
        P("rep"),
        P("rep", None),
        P("rep", None, None, None),
        P("rep", None, None),
        P("rep", None, None),
    )
    out_specs = P("rep", None, "ctx", None)
    return jax.shard_map(body, mesh=mesh, in_specs=in_specs, out_specs=out_specs, check_vma=False)
```

```python
import functools

import jax
import jax.numpy as jnp
import numpy as np
from jax import lax
from jax.experimental import pallas as pl
from jax.experimental.pallas import tpu as pltpu
from jax.sharding import PartitionSpec as P

score_scale = 192.0 ** (-0.5)
masked = -1e30
MESH = pl.DeviceIdType.MESH
F32 = jnp.float32
BF16 = jnp.bfloat16


def nt(a, b):
    return lax.dot_general(a, b, (((1,), (1,)), ((), ())), preferred_element_type=F32)


def nn(a, b):
    return lax.dot_general(a, b, (((1,), (0,)), ((), ())), preferred_element_type=F32)


def iota(shape, dim):
    return lax.broadcasted_iota(jnp.int32, shape, dim)


def spread_heads(pairs):
    n = pairs.shape[0]
    row, col = iota((2 * n, n), 0), iota((2 * n, n), 1)
    pick = jnp.where(col == (row >> 1), 1.0, 0.0).astype(BF16)
    both = nn(pick, pairs)
    row, lane = iota((2 * n, 128), 0), iota((2 * n, 128), 1)
    one = jnp.where((lane >> 6) == (row & 1), both, 0.0)
    return (one + pltpu.roll(one, 64, 1)).astype(BF16)


def stats_block(top, total):
    lane = iota((top.shape[0], 128), 1)
    block = jnp.zeros((top.shape[0], 128), F32)
    for at, value, terms in ((0, top, 3), (3, total, 2)):
        for n in range(terms):
            term = value.astype(BF16).astype(F32)
            block = jnp.where(lane == at + n, term, block)
            value = value - term
    return block.astype(BF16)


def read_stats(block):
    block = block.astype(F32)
    return block[:, 0:1] + block[:, 1:2] + block[:, 2:3], block[:, 3:4] + block[:, 4:5]


def kernel(
    n_rep,
    tab_hbm,
    len_hbm,
    mov_hbm,
    lat_hbm,
    rope_hbm,
    q_hbm,
    qr_hbm,
    nk_hbm,
    out,
    keys,
    rope_v,
    q_v,
    qown,
    qr_v,
    nk_v,
    xq,
    xk,
    nkx,
    nkf,
    msg,
    nkmsg,
    nkgot,
    qall,
    pages,
    got,
    pages_t,
    got_t,
    psend,
    precv,
    own,
    ownstat,
    rs,
    rr,
    ms,
    mr,
    newp,
    newstat,
    ysend,
    res,
    tab_s,
    len_s,
    mov_s,
    in_sem,
    y_s,
    y_r,
    ag_s,
    ag_r,
    k_s,
    k_r,
    p_s,
    p_r,
    r_s,
    r_r,
    m_s,
    m_r,
    o_s,
    o_r,
):
    rep = lax.axis_index("rep")
    ctx = lax.axis_index("ctx")
    cx = ctx // 2
    core = ctx % 2
    partner = {"rep": (rep + n_rep // 2) % n_rep, "ctx": ctx}
    other = cx * 2 + (1 - core)
    sibling = {"rep": rep, "ctx": other}

    def chip(d):
        return {"rep": rep, "ctx": ((cx + d) % 4) * 2 + core}

    barrier = pltpu.get_barrier_semaphore()
    for peer in (partner, chip(2), chip(1), chip(3), sibling):
        pl.semaphore_signal(barrier, inc=1, device_id=peer, device_id_type=MESH)

    loads = {}

    def load(name, src, dst):
        copy = pltpu.make_async_copy(src, dst, in_sem.at[len(loads)])
        copy.start()
        loads[name] = copy

    load("plan", tab_hbm, tab_s)
    load("moves", mov_hbm, mov_s)
    load("lengths", len_hbm, len_s)
    load("qr", qr_hbm, qr_v)
    for s in range(2):
        load(("own", s), q_hbm.at[:, s, pl.ds(pl.multiple_of(ctx * 16, 16), 16), :], qown.at[:, s])
    load("nk", nk_hbm, nk_v)
    load("rope", rope_hbm, rope_v)
    for i in range(4):
        load(("lat", i), lat_hbm.at[i], keys.at[i, :, 0:512])
    for g in range(8):
        c = (core + g // 4) % 2
        head = pl.multiple_of(((g % 4) * 2 + c) * 16, 16)
        for s in range(2):
            load(("q", g, s), q_hbm.at[:, s, pl.ds(head, 16), :], q_v.at[:, g, s])

    def remote(src, dst, send_sem, recv_sem, device):
        copy = pltpu.make_async_remote_copy(
            src_ref=src,
            dst_ref=dst,
            send_sem=send_sem,
            recv_sem=recv_sem,
            device_id=device,
            device_id_type=MESH,
        )
        copy.start()
        return copy

    half = (slice(0, 640), slice(640, 1152))
    whole = slice(0, 1152)
    asked = [(k, part) for k in range(2) for part in half]
    summed = [(k, part) for k in range(2) for part in half]

    def rows_of(block):
        rot = block[:, 512:640].astype(F32)
        lane = iota(rot.shape, 1)
        rots = []
        for s in range(2):
            one = jnp.where((lane >> 6) == s, rot, 0.0)
            rots.append((one + pltpu.roll(one, 64, 1)).astype(BF16))
        latent = jnp.concatenate([block[:, 0:512], block[:, 640:1152]], axis=0)
        return jnp.concatenate([latent, jnp.concatenate(rots, axis=0)], axis=1)

    loads["qr"].wait()
    for i in range(4):
        rows = qr_v[i].astype(F32)
        for b in range(64):
            j = b // 8
            at = ((j % 2) * 4 + j // 2) * 16 + b % 8
            for s in range(2):
                xq[i, at + 8 * s : at + 8 * s + 1, :] = rows[s : s + 1, 128 * b : 128 * b + 128]

    for name in ("plan", "lengths", "moves"):
        loads[name].wait()
    row = (mov_s[0, 0] * 4 + mov_s[0, 1]) * 8
    slots = [tab_s[row + i] for i in range(4)]
    places = [tab_s[row + 4 + b] for b in range(4)]

    def pairs_of(slot, c):
        return xq[slot, pl.ds(pl.multiple_of(c * 64, 64), 64), :].astype(BF16)

    def own_pairs(slot):
        return xq[slot, pl.ds(pl.multiple_of(core * 64 + cx * 16, 16), 16), :].astype(BF16)

    for name in (("own", 0), ("own", 1), "nk"):
        loads[name].wait()
    nkx[...] = jnp.zeros_like(nkx)
    for k in range(2):
        slot = slots[2 + k]
        msg[k, :, 0:512] = qown[slot, 0]
        msg[k, :, 640:1152] = qown[slot, 1]
        rot = spread_heads(own_pairs(slot))
        lane = iota((16, 128), 1)
        msg[k, :, 512:640] = jnp.where(lane < 64, rot[0:16], rot[16:32])
        fresh = nk_v[slot].astype(F32)
        for n in range(2):
            for u in range(4):
                nkx[n * 4 + u : n * 4 + u + 1, :] = fresh[n : n + 1, 128 * u : 128 * u + 128]
            nkx[8 + n : 9 + n, 0:64] = fresh[n : n + 1, 512:576]
        nkmsg[k] = nkx[...].astype(BF16)

    def rope_keys():
        loads["rope"].wait()
        for page in range(12):
            rows = rope_v[page].astype(F32)
            for c in range(32):
                for i in range(4):
                    at = page * 32 + c
                    xk[i, at : at + 1, :] = rows[i : i + 1, c * 128 : c * 128 + 128]
        token, col = iota((768, 384), 0), iota((768, 384), 1)
        pick = jnp.where(col == (token >> 1), 1.0, 0.0).astype(BF16)
        token, lane = iota((768, 128), 0), iota((768, 128), 1)
        keep = (lane >> 6) == (token & 1)
        both = nn(pick, jnp.concatenate([xk[i].astype(BF16) for i in range(4)], axis=1))
        for i in range(4):
            keys[i, :, 512:640] = jnp.where(keep, both[:, i * 128 : i * 128 + 128], 0.0).astype(BF16)
        for i in range(4):
            loads[("lat", i)].wait()
        for k in range(2):
            pages[k] = keys[slots[2 + k]]

    def attend(q, held, group, length, turned=None):
        score = (nt(q, held) if turned is None else nn(q, turned[...])) * score_scale
        valid = group * 768 + iota((1, 768), 1) < length
        score = jnp.where(valid, score, masked)
        top = jnp.max(score, axis=1, keepdims=True)
        weights = jnp.where(valid, jnp.exp(score - top), 0.0)
        total = jnp.sum(weights, axis=1, keepdims=True)
        return nn(weights.astype(BF16), held[:, 0:512]).astype(BF16), top, total

    def stay(i):
        slot = slots[i]
        pairs = jnp.concatenate([pairs_of(slot, core), pairs_of(slot, 1 - core)], axis=0)
        q = jnp.concatenate([q_v[slot].reshape(256, 512), spread_heads(pairs)], axis=1)
        part, top, total = attend(q, keys[slot], ctx, len_s[slot])
        psend[i, :, 0:512] = part[128:256]
        psend[i, :, 512:640] = stats_block(top[128:256], total[128:256])
        own[i] = part[0:128]
        lane = iota((128, 128), 1)
        ownstat[i] = jnp.where(lane == 0, top[0:128], total[0:128])

    def add(a, b):
        part_a, top_a, total_a = a
        part_b, top_b, total_b = b
        top = jnp.maximum(top_a, top_b)
        scale_a, scale_b = jnp.exp(top_a - top), jnp.exp(top_b - top)
        part = scale_a * part_a.astype(F32) + scale_b * part_b.astype(F32)
        return part.astype(BF16), stats_block(top, scale_a * total_a + scale_b * total_b)

    def scatter_stay(i):
        chips[i] = [
            remote(rs.at[i, (cx + d) % 4], rr.at[i, cx], r_s.at[i, d], r_r.at[i, d], chip(d))
            for d in (2, 1, 3)
        ]

    def scatter_moved(k, total):
        part, stats = total
        sent, got = ms.at[k], mr.at[k]
        for s, at in ((0, slice(0, 512)), (1, slice(640, 1152))):
            sent[:, :, at] = part[64 * s : 64 * s + 64].reshape(4, 16, 512)
        lane = iota((64, 128), 1)
        stats = jnp.where(lane < 64, stats[0:64].astype(F32), pltpu.roll(stats[64:128].astype(F32), 64, 1))
        sent[:, :, 512:640] = stats.astype(BF16).reshape(4, 16, 128)
        copies = []
        for n, (kk, part) in enumerate(summed):
            if kk == k:
                copies.append([])
                for d in (2, 1, 3):
                    src, dst = sent.at[(cx + d) % 4, :, part], got.at[cx, :, part]
                    copies[-1].append(remote(src, dst, m_s.at[n, d], m_r.at[n, d], chip(d)))
        got[cx] = sent[cx]
        return copies

    def merge_moved(k, s):
        at = slice(0, 512) if s == 0 else slice(640, 1152)
        here = slice(16 * s, 16 * s + 16)
        stats = [read_stats(mr[k, c, :, 512 + 64 * s : 640]) for c in range(4)]
        parts = [mr[k, c, :, at].astype(F32) for c in range(4)]
        stats.append((newstat[2 + k, here, 0:1], newstat[2 + k, here, 1:2]))
        parts.append(newp[2 + k, here])
        return combine(parts, stats)

    def merge_cores(i):
        pairs[i].wait()
        top, total = read_stats(precv[i, :, 512:640])
        mine = (own[i], ownstat[i, :, 0:1], ownstat[i, :, 1:2])
        part, stats = add(mine, (precv[i, :, 0:512], top, total))
        rs[i, :, :, 0:512] = part.reshape(4, 32, 512)
        rs[i, :, :, 512:640] = stats.reshape(4, 32, 128)
        rr[i, cx] = rs[i, cx]

    def merge_chips(copies, got, fresh, fresh_stat):
        for copy in copies:
            copy.wait_recv()
        blocks = [got[c] for c in range(4)]
        parts = [b[:, 0:512].astype(F32) for b in blocks] + [fresh]
        stats = [read_stats(b[:, 512:640]) for b in blocks]
        stats.append((fresh_stat[:, 0:1], fresh_stat[:, 1:2]))
        return combine(parts, stats)

    def combine(parts, stats):
        top = functools.reduce(jnp.maximum, [t for t, _ in stats])
        factors = [jnp.exp(t - top) for t, _ in stats]
        numer = sum(f * p for f, p in zip(factors, parts))
        denom = sum(f * t for f, (_, t) in zip(factors, stats))
        return (numer / denom).astype(BF16)

    def new_tokens():
        nkf[...] = jnp.zeros_like(nkf)
        for i in range(2):
            nkf[2 * i : 2 * i + 2, 0:576] = nk_v[slots[i]].astype(F32)
        for k in range(2):
            fresh = nkgot[k].astype(F32)
            for n in range(2):
                at = 4 + 2 * k + n
                for u in range(4):
                    nkf[at : at + 1, 128 * u : 128 * u + 128] = fresh[n * 4 + u : n * 4 + u + 1, :]
                nkf[at : at + 1, 512:576] = fresh[8 + n : 9 + n, 0:64]
        fresh = nkf[...].astype(BF16)
        queries = [
            jnp.concatenate([qown[slots[i]].reshape(32, 512), spread_heads(own_pairs(slots[i]))], axis=1)
            for i in range(2)
        ]
        queries = jnp.concatenate(queries + [rows_of(qall[k, cx]) for k in range(2)], axis=0)
        score = nt(queries, fresh) * score_scale
        row, col = iota((128, 128), 0), iota((128, 128), 1)
        valid = ((row >> 5) == (col >> 1)) & ((col & 1) <= ((row >> 4) & 1))
        score = jnp.where(valid, score, masked)
        top = jnp.max(score, axis=1, keepdims=True)
        weights = jnp.where(valid, jnp.exp(score - top), 0.0)
        total = jnp.sum(weights, axis=1, keepdims=True)
        newp[...] = nn(weights.astype(BF16), fresh[:, 0:512]).reshape(4, 32, 512)
        newstat[...] = jnp.where(col == 0, top, total).reshape(4, 32, 128)

    pairs = [None] * 2
    chips = [None] * 2

    rope_keys()
    for g in range(8):
        for s in range(2):
            loads[("q", g, s)].wait()
    pl.semaphore_wait(barrier, 5)
    y_out = []
    for n, (k, part) in enumerate(asked):
        src, dst = msg.at[k, :, part], qall.at[k, cx, :, part]
        y_out.append(remote(src, dst, y_s.at[n], y_r.at[n], partner))
    y_out.append(remote(nkmsg, nkgot, y_s.at[4], y_r.at[4], partner))
    for i in (0, 1):
        stay(i)
        pairs[i] = remote(psend.at[i], precv.at[i], p_s.at[i], p_r.at[i], sibling)
    for k in range(2):
        pages_t[k] = pages[k].T
    page_out = [remote(pages.at[k, :, 0:512], got.at[k], k_s.at[k], k_r.at[k], sibling) for k in range(2)]
    turned_out = [remote(pages_t.at[k], got_t.at[k], k_s.at[2 + k], k_r.at[2 + k], sibling) for k in range(2)]
    gathers = []
    for n, (k, part) in enumerate(asked):
        y_out[n].wait_recv()
        block = qall.at[k, cx, :, part]
        gathers.append([remote(block, block, ag_s.at[n, d], ag_r.at[n, d], chip(d)) for d in (2, 1, 3)])
    y_out[-1].wait_recv()
    new_tokens()
    for i in range(2):
        merge_cores(i)

    sums = []
    for k in range(2):
        length = len_s[slots[2 + k]]
        page_out[k].wait_recv()
        turned_out[k].wait_recv()
        for n, (kk, _) in enumerate(asked):
            if kk == k:
                for copy in gathers[n]:
                    copy.wait_recv()
        q = rows_of(qall[k].reshape(64, 1152))
        total = add(attend(q, pages[k], ctx, length, pages_t.at[k]), attend(q, got[k], other, length, got_t.at[k]))
        sums.append(scatter_moved(k, total))
    scatter_stay(0)
    scatter_stay(1)

    home = []
    for k in range(2):
        for s in range(2):
            if s < len(sums[k]):
                for copy in sums[k][s]:
                    copy.wait_recv()
            at = slice(16 * s, 16 * s + 16)
            ysend[k, at] = merge_moved(k, s)
            n = 2 * k + s
            if 2 == 2:
                home.append(remote(ysend.at[k, at], res.at[2 + k, at], o_s.at[n], o_r.at[n], partner))
        if 2 == 1:
            home.append(remote(ysend.at[k], res.at[2 + k], o_s.at[k], o_r.at[k], partner))
    for i in range(2):
        res[i] = merge_chips(chips[i], rr.at[i], newp[i], newstat[i])

    for copy in sum(gathers + sum(sums, []) + chips, y_out + page_out + turned_out):
        copy.wait_send()
    for copy in home:
        copy.wait()

    for b in range(4):
        out[b] = res[places[b]]


def plan_table():
    rows = np.zeros((4, 4, 8), np.int32)
    for first in range(4):
        for second in range(4):
            stay = [b for b in range(4) if b not in (first, second)]
            slots = (stay + [first, second])[:4] if first != second else [0, 1, 2, 3]
            rows[first, second, :4] = slots
            rows[first, second, 4:] = [slots.index(b) for b in range(4)]
    return rows.reshape(128)


def body(cache_latent, cache_rope, lengths, move_slots, q_latent, q_rope, new_keys):
    dma = pltpu.SemaphoreType.DMA
    hbm = pl.BlockSpec(memory_space=pltpu.HBM)
    out = pl.pallas_call(
        functools.partial(kernel, lax.axis_size("rep")),
        out_shape=jax.ShapeDtypeStruct((4, 32, 512), BF16),
        in_specs=[hbm] * 8,
        out_specs=pl.BlockSpec(memory_space=pltpu.VMEM),
        scratch_shapes=[
            pltpu.VMEM((4, 768, 640), BF16),
            pltpu.VMEM((12, 4, 4096), BF16),
            pltpu.VMEM((4, 8, 2, 16, 512), BF16),
            pltpu.VMEM((4, 2, 16, 512), BF16),
            pltpu.VMEM((4, 2, 8192), BF16),
            pltpu.VMEM((4, 2, 576), BF16),
            pltpu.VMEM((4, 128, 128), F32),
            pltpu.VMEM((4, 384, 128), F32),
            pltpu.VMEM((16, 128), F32),
            pltpu.VMEM((128, 640), F32),
            pltpu.VMEM((2, 16, 1152), BF16),
            pltpu.VMEM((2, 16, 128), BF16),
            pltpu.VMEM((2, 16, 128), BF16),
            pltpu.VMEM((2, 4, 16, 1152), BF16),
            pltpu.VMEM((2, 768, 640), BF16),
            pltpu.VMEM((2, 768, 512), BF16),
            pltpu.VMEM((2, 640, 768), BF16),
            pltpu.VMEM((2, 640, 768), BF16),
            pltpu.VMEM((2, 128, 640), BF16),
            pltpu.VMEM((2, 128, 640), BF16),
            pltpu.VMEM((2, 128, 512), BF16),
            pltpu.VMEM((2, 128, 128), F32),
            pltpu.VMEM((2, 4, 32, 640), BF16),
            pltpu.VMEM((2, 4, 32, 640), BF16),
            pltpu.VMEM((2, 4, 16, 1152), BF16),
            pltpu.VMEM((2, 4, 16, 1152), BF16),
            pltpu.VMEM((4, 32, 512), F32),
            pltpu.VMEM((4, 32, 128), F32),
            pltpu.VMEM((2, 32, 512), BF16),
            pltpu.VMEM((4, 32, 512), BF16),
            pltpu.SMEM((128,), jnp.int32),
            pltpu.SMEM((4,), jnp.int32),
            pltpu.SMEM((1, 2), jnp.int32),
            dma((32,)),
            dma((5,)),
            dma((5,)),
            dma((4, 4)),
            dma((4, 4)),
            dma((4,)),
            dma((4,)),
            dma((2,)),
            dma((2,)),
            dma((2, 4)),
            dma((2, 4)),
            dma((4, 4)),
            dma((4, 4)),
            dma((4,)),
            dma((4,)),
        ],
        compiler_params=pltpu.CompilerParams(
            collective_id=0, has_side_effects=True, vmem_limit_bytes=48 * 1024 * 1024
        ),
        cost_estimate=pl.CostEstimate(flops=1800000000, bytes_accessed=4800000, transcendentals=800000),
    )(
        *[
            pltpu.with_memory_space_constraint(x, pltpu.HBM)
            for x in (
                jnp.asarray(plan_table()),
                lengths,
                move_slots,
                cache_latent.reshape(4, 768, 512),
                cache_rope.transpose(1, 0, 2),
                q_latent,
                q_rope,
                new_keys,
            )
        ]
    )
    return out.reshape(4, 2, 16, 512)


def solution(mesh):
    in_specs = (
        P("rep", "ctx", None, None),
        P("rep", "ctx", None),
        P("rep"),
        P("rep", None),
        P("rep", None, None, None),
        P("rep", None, None),
        P("rep", None, None),
    )
    out_specs = P("rep", None, "ctx", None)
    return jax.shard_map(body, mesh=mesh, in_specs=in_specs, out_specs=out_specs, check_vma=False)
```

```python
import functools

import jax
import jax.numpy as jnp
import numpy as np
from jax import lax
from jax.experimental import pallas as pl
from jax.experimental.pallas import tpu as pltpu
from jax.sharding import PartitionSpec as P

score_scale = 192.0 ** (-0.5)
masked = -1e30
MESH = pl.DeviceIdType.MESH
F32 = jnp.float32
BF16 = jnp.bfloat16


def nt(a, b):
    return lax.dot_general(a, b, (((1,), (1,)), ((), ())), preferred_element_type=F32)


def nn(a, b):
    return lax.dot_general(a, b, (((1,), (0,)), ((), ())), preferred_element_type=F32)


def iota(shape, dim):
    return lax.broadcasted_iota(jnp.int32, shape, dim)


def spread_heads(pairs):
    n = pairs.shape[0]
    row, col = iota((2 * n, n), 0), iota((2 * n, n), 1)
    pick = jnp.where(col == (row >> 1), 1.0, 0.0).astype(BF16)
    both = nn(pick, pairs)
    row, lane = iota((2 * n, 128), 0), iota((2 * n, 128), 1)
    one = jnp.where((lane >> 6) == (row & 1), both, 0.0)
    return (one + pltpu.roll(one, 64, 1)).astype(BF16)


def stats_block(top, total):
    lane = iota((top.shape[0], 128), 1)
    block = jnp.zeros((top.shape[0], 128), F32)
    for at, value, terms in ((0, top, 3), (3, total, 2)):
        for n in range(terms):
            term = value.astype(BF16).astype(F32)
            block = jnp.where(lane == at + n, term, block)
            value = value - term
    return block.astype(BF16)


def read_stats(block):
    block = block.astype(F32)
    return block[:, 0:1] + block[:, 1:2] + block[:, 2:3], block[:, 3:4] + block[:, 4:5]


def kernel(
    n_rep,
    tab_hbm,
    len_hbm,
    mov_hbm,
    lat_hbm,
    rope_hbm,
    q_hbm,
    qr_hbm,
    nk_hbm,
    out,
    keys,
    rope_v,
    q_v,
    qown,
    qr_v,
    nk_v,
    xq,
    xk,
    nkx,
    nkf,
    msg,
    nkmsg,
    nkgot,
    qall,
    pages,
    got,
    pages_t,
    got_t,
    psend,
    precv,
    own,
    ownstat,
    rs,
    rr,
    ms,
    mr,
    newp,
    newstat,
    ysend,
    res,
    tab_s,
    len_s,
    mov_s,
    in_sem,
    y_s,
    y_r,
    ag_s,
    ag_r,
    k_s,
    k_r,
    p_s,
    p_r,
    r_s,
    r_r,
    m_s,
    m_r,
    o_s,
    o_r,
):
    rep = lax.axis_index("rep")
    ctx = lax.axis_index("ctx")
    cx = ctx // 2
    core = ctx % 2
    partner = {"rep": (rep + n_rep // 2) % n_rep, "ctx": ctx}
    other = cx * 2 + (1 - core)
    sibling = {"rep": rep, "ctx": other}

    def chip(d):
        return {"rep": rep, "ctx": ((cx + d) % 4) * 2 + core}

    barrier = pltpu.get_barrier_semaphore()
    for peer in (partner, chip(2), chip(1), chip(3), sibling):
        pl.semaphore_signal(barrier, inc=1, device_id=peer, device_id_type=MESH)

    loads = {}

    def load(name, src, dst):
        copy = pltpu.make_async_copy(src, dst, in_sem.at[len(loads)])
        copy.start()
        loads[name] = copy

    load("plan", tab_hbm, tab_s)
    load("moves", mov_hbm, mov_s)
    load("lengths", len_hbm, len_s)
    load("qr", qr_hbm, qr_v)
    for s in range(2):
        load(("own", s), q_hbm.at[:, s, pl.ds(pl.multiple_of(ctx * 16, 16), 16), :], qown.at[:, s])
    load("nk", nk_hbm, nk_v)
    load("rope", rope_hbm, rope_v)
    for i in range(4):
        load(("lat", i), lat_hbm.at[i], keys.at[i, :, 0:512])
    for g in range(8):
        c = (core + g // 4) % 2
        head = pl.multiple_of(((g % 4) * 2 + c) * 16, 16)
        for s in range(2):
            load(("q", g, s), q_hbm.at[:, s, pl.ds(head, 16), :], q_v.at[:, g, s])

    def remote(src, dst, send_sem, recv_sem, device):
        copy = pltpu.make_async_remote_copy(
            src_ref=src,
            dst_ref=dst,
            send_sem=send_sem,
            recv_sem=recv_sem,
            device_id=device,
            device_id_type=MESH,
        )
        copy.start()
        return copy

    half = (slice(0, 640), slice(640, 1152))
    whole = slice(0, 1152)
    asked = [(k, part) for k in range(2) for part in half]
    summed = [(k, part) for k in range(2) for part in half]

    def rows_of(block):
        rot = block[:, 512:640].astype(F32)
        lane = iota(rot.shape, 1)
        rots = []
        for s in range(2):
            one = jnp.where((lane >> 6) == s, rot, 0.0)
            rots.append((one + pltpu.roll(one, 64, 1)).astype(BF16))
        latent = jnp.concatenate([block[:, 0:512], block[:, 640:1152]], axis=0)
        return jnp.concatenate([latent, jnp.concatenate(rots, axis=0)], axis=1)

    loads["qr"].wait()
    for i in range(4):
        rows = qr_v[i].astype(F32)
        for b in range(64):
            j = b // 8
            at = ((j % 2) * 4 + j // 2) * 16 + b % 8
            for s in range(2):
                xq[i, at + 8 * s : at + 8 * s + 1, :] = rows[s : s + 1, 128 * b : 128 * b + 128]

    for name in ("plan", "lengths", "moves"):
        loads[name].wait()
    row = (mov_s[0, 0] * 4 + mov_s[0, 1]) * 8
    slots = [tab_s[row + i] for i in range(4)]
    places = [tab_s[row + 4 + b] for b in range(4)]

    def pairs_of(slot, c):
        return xq[slot, pl.ds(pl.multiple_of(c * 64, 64), 64), :].astype(BF16)

    def own_pairs(slot):
        return xq[slot, pl.ds(pl.multiple_of(core * 64 + cx * 16, 16), 16), :].astype(BF16)

    for name in (("own", 0), ("own", 1), "nk"):
        loads[name].wait()
    nkx[...] = jnp.zeros_like(nkx)
    for k in range(2):
        slot = slots[2 + k]
        msg[k, :, 0:512] = qown[slot, 0]
        msg[k, :, 640:1152] = qown[slot, 1]
        rot = spread_heads(own_pairs(slot))
        lane = iota((16, 128), 1)
        msg[k, :, 512:640] = jnp.where(lane < 64, rot[0:16], rot[16:32])
        fresh = nk_v[slot].astype(F32)
        for n in range(2):
            for u in range(4):
                nkx[n * 4 + u : n * 4 + u + 1, :] = fresh[n : n + 1, 128 * u : 128 * u + 128]
            nkx[8 + n : 9 + n, 0:64] = fresh[n : n + 1, 512:576]
        nkmsg[k] = nkx[...].astype(BF16)

    def rope_keys():
        loads["rope"].wait()
        for page in range(12):
            rows = rope_v[page].astype(F32)
            for c in range(32):
                for i in range(4):
                    at = page * 32 + c
                    xk[i, at : at + 1, :] = rows[i : i + 1, c * 128 : c * 128 + 128]
        token, col = iota((768, 384), 0), iota((768, 384), 1)
        pick = jnp.where(col == (token >> 1), 1.0, 0.0).astype(BF16)
        token, lane = iota((768, 128), 0), iota((768, 128), 1)
        keep = (lane >> 6) == (token & 1)
        both = nn(pick, jnp.concatenate([xk[i].astype(BF16) for i in range(4)], axis=1))
        for i in range(4):
            keys[i, :, 512:640] = jnp.where(keep, both[:, i * 128 : i * 128 + 128], 0.0).astype(BF16)
        for i in range(4):
            loads[("lat", i)].wait()
        for k in range(2):
            pages[k] = keys[slots[2 + k]]

    def attend(q, held, group, length, turned=None):
        score = (nt(q, held) if turned is None else nn(q, turned[...])) * score_scale
        valid = group * 768 + iota((1, 768), 1) < length
        score = jnp.where(valid, score, masked)
        top = jnp.max(score, axis=1, keepdims=True)
        weights = jnp.where(valid, jnp.exp(score - top), 0.0)
        total = jnp.sum(weights, axis=1, keepdims=True)
        return nn(weights.astype(BF16), held[:, 0:512]).astype(BF16), top, total

    def stay(i):
        slot = slots[i]
        pairs = jnp.concatenate([pairs_of(slot, core), pairs_of(slot, 1 - core)], axis=0)
        q = jnp.concatenate([q_v[slot].reshape(256, 512), spread_heads(pairs)], axis=1)
        part, top, total = attend(q, keys[slot], ctx, len_s[slot])
        psend[i, :, 0:512] = part[128:256]
        psend[i, :, 512:640] = stats_block(top[128:256], total[128:256])
        own[i] = part[0:128]
        lane = iota((128, 128), 1)
        ownstat[i] = jnp.where(lane == 0, top[0:128], total[0:128])

    def add(a, b):
        part_a, top_a, total_a = a
        part_b, top_b, total_b = b
        top = jnp.maximum(top_a, top_b)
        scale_a, scale_b = jnp.exp(top_a - top), jnp.exp(top_b - top)
        part = scale_a * part_a.astype(F32) + scale_b * part_b.astype(F32)
        return part.astype(BF16), stats_block(top, scale_a * total_a + scale_b * total_b)

    def scatter_stay(i):
        chips[i] = [
            remote(rs.at[i, (cx + d) % 4], rr.at[i, cx], r_s.at[i, d], r_r.at[i, d], chip(d))
            for d in (2, 1, 3)
        ]

    def scatter_moved(k, total):
        part, stats = total
        sent, got = ms.at[k], mr.at[k]
        for s, at in ((0, slice(0, 512)), (1, slice(640, 1152))):
            sent[:, :, at] = part[64 * s : 64 * s + 64].reshape(4, 16, 512)
        lane = iota((64, 128), 1)
        stats = jnp.where(lane < 64, stats[0:64].astype(F32), pltpu.roll(stats[64:128].astype(F32), 64, 1))
        sent[:, :, 512:640] = stats.astype(BF16).reshape(4, 16, 128)
        copies = []
        for n, (kk, part) in enumerate(summed):
            if kk == k:
                copies.append([])
                for d in (2, 1, 3):
                    src, dst = sent.at[(cx + d) % 4, :, part], got.at[cx, :, part]
                    copies[-1].append(remote(src, dst, m_s.at[n, d], m_r.at[n, d], chip(d)))
        got[cx] = sent[cx]
        return copies

    def merge_moved(k, s):
        at = slice(0, 512) if s == 0 else slice(640, 1152)
        here = slice(16 * s, 16 * s + 16)
        stats = [read_stats(mr[k, c, :, 512 + 64 * s : 640]) for c in range(4)]
        parts = [mr[k, c, :, at].astype(F32) for c in range(4)]
        stats.append((newstat[2 + k, here, 0:1], newstat[2 + k, here, 1:2]))
        parts.append(newp[2 + k, here])
        return combine(parts, stats)

    def merge_cores(i):
        pairs[i].wait()
        top, total = read_stats(precv[i, :, 512:640])
        mine = (own[i], ownstat[i, :, 0:1], ownstat[i, :, 1:2])
        part, stats = add(mine, (precv[i, :, 0:512], top, total))
        rs[i, :, :, 0:512] = part.reshape(4, 32, 512)
        rs[i, :, :, 512:640] = stats.reshape(4, 32, 128)
        rr[i, cx] = rs[i, cx]

    def merge_chips(copies, got, fresh, fresh_stat):
        for copy in copies:
            copy.wait_recv()
        blocks = [got[c] for c in range(4)]
        parts = [b[:, 0:512].astype(F32) for b in blocks] + [fresh]
        stats = [read_stats(b[:, 512:640]) for b in blocks]
        stats.append((fresh_stat[:, 0:1], fresh_stat[:, 1:2]))
        return combine(parts, stats)

    def combine(parts, stats):
        top = functools.reduce(jnp.maximum, [t for t, _ in stats])
        factors = [jnp.exp(t - top) for t, _ in stats]
        numer = sum(f * p for f, p in zip(factors, parts))
        denom = sum(f * t for f, (_, t) in zip(factors, stats))
        return (numer / denom).astype(BF16)

    def new_tokens():
        nkf[...] = jnp.zeros_like(nkf)
        for i in range(2):
            nkf[2 * i : 2 * i + 2, 0:576] = nk_v[slots[i]].astype(F32)
        for k in range(2):
            fresh = nkgot[k].astype(F32)
            for n in range(2):
                at = 4 + 2 * k + n
                for u in range(4):
                    nkf[at : at + 1, 128 * u : 128 * u + 128] = fresh[n * 4 + u : n * 4 + u + 1, :]
                nkf[at : at + 1, 512:576] = fresh[8 + n : 9 + n, 0:64]
        fresh = nkf[...].astype(BF16)
        queries = [
            jnp.concatenate([qown[slots[i]].reshape(32, 512), spread_heads(own_pairs(slots[i]))], axis=1)
            for i in range(2)
        ]
        queries = jnp.concatenate(queries + [rows_of(qall[k, cx]) for k in range(2)], axis=0)
        score = nt(queries, fresh) * score_scale
        row, col = iota((128, 128), 0), iota((128, 128), 1)
        valid = ((row >> 5) == (col >> 1)) & ((col & 1) <= ((row >> 4) & 1))
        score = jnp.where(valid, score, masked)
        top = jnp.max(score, axis=1, keepdims=True)
        weights = jnp.where(valid, jnp.exp(score - top), 0.0)
        total = jnp.sum(weights, axis=1, keepdims=True)
        newp[...] = nn(weights.astype(BF16), fresh[:, 0:512]).reshape(4, 32, 512)
        newstat[...] = jnp.where(col == 0, top, total).reshape(4, 32, 128)

    pairs = [None] * 2
    chips = [None] * 2

    rope_keys()
    for g in range(8):
        for s in range(2):
            loads[("q", g, s)].wait()
    pl.semaphore_wait(barrier, 5)
    y_out = []
    for n, (k, part) in enumerate(asked):
        src, dst = msg.at[k, :, part], qall.at[k, cx, :, part]
        y_out.append(remote(src, dst, y_s.at[n], y_r.at[n], partner))
    y_out.append(remote(nkmsg, nkgot, y_s.at[4], y_r.at[4], partner))
    for i in (0, 1):
        stay(i)
        pairs[i] = remote(psend.at[i], precv.at[i], p_s.at[i], p_r.at[i], sibling)
    for k in range(2):
        pages_t[k] = pages[k].T
    page_out = [remote(pages.at[k, :, 0:512], got.at[k], k_s.at[k], k_r.at[k], sibling) for k in range(2)]
    turned_out = [remote(pages_t.at[k], got_t.at[k], k_s.at[2 + k], k_r.at[2 + k], sibling) for k in range(2)]
    for i in range(2):
        merge_cores(i)
    scatter_stay(0)
    gathers = []
    for n, (k, part) in enumerate(asked):
        y_out[n].wait_recv()
        block = qall.at[k, cx, :, part]
        gathers.append([remote(block, block, ag_s.at[n, d], ag_r.at[n, d], chip(d)) for d in (2, 1, 3)])
    y_out[-1].wait_recv()
    new_tokens()

    sums = []
    for k in range(2):
        length = len_s[slots[2 + k]]
        page_out[k].wait_recv()
        turned_out[k].wait_recv()
        for n, (kk, _) in enumerate(asked):
            if kk == k:
                for copy in gathers[n]:
                    copy.wait_recv()
        q = rows_of(qall[k].reshape(64, 1152))
        total = add(attend(q, pages[k], ctx, length, pages_t.at[k]), attend(q, got[k], other, length, got_t.at[k]))
        sums.append(scatter_moved(k, total))

    home = []
    for k in range(2):
        for s in range(2):
            if s < len(sums[k]):
                for copy in sums[k][s]:
                    copy.wait_recv()
            at = slice(16 * s, 16 * s + 16)
            ysend[k, at] = merge_moved(k, s)
            n = 2 * k + s
            if 2 == 2:
                home.append(remote(ysend.at[k, at], res.at[2 + k, at], o_s.at[n], o_r.at[n], partner))
        if 2 == 1:
            home.append(remote(ysend.at[k], res.at[2 + k], o_s.at[k], o_r.at[k], partner))
    scatter_stay(1)
    for i in range(2):
        res[i] = merge_chips(chips[i], rr.at[i], newp[i], newstat[i])

    for copy in sum(gathers + sum(sums, []) + chips, y_out + page_out + turned_out):
        copy.wait_send()
    for copy in home:
        copy.wait()

    for b in range(4):
        out[b] = res[places[b]]


def plan_table():
    rows = np.zeros((4, 4, 8), np.int32)
    for first in range(4):
        for second in range(4):
            stay = [b for b in range(4) if b not in (first, second)]
            slots = (stay + [first, second])[:4] if first != second else [0, 1, 2, 3]
            rows[first, second, :4] = slots
            rows[first, second, 4:] = [slots.index(b) for b in range(4)]
    return rows.reshape(128)


def body(cache_latent, cache_rope, lengths, move_slots, q_latent, q_rope, new_keys):
    dma = pltpu.SemaphoreType.DMA
    hbm = pl.BlockSpec(memory_space=pltpu.HBM)
    out = pl.pallas_call(
        functools.partial(kernel, lax.axis_size("rep")),
        out_shape=jax.ShapeDtypeStruct((4, 32, 512), BF16),
        in_specs=[hbm] * 8,
        out_specs=pl.BlockSpec(memory_space=pltpu.VMEM),
        scratch_shapes=[
            pltpu.VMEM((4, 768, 640), BF16),
            pltpu.VMEM((12, 4, 4096), BF16),
            pltpu.VMEM((4, 8, 2, 16, 512), BF16),
            pltpu.VMEM((4, 2, 16, 512), BF16),
            pltpu.VMEM((4, 2, 8192), BF16),
            pltpu.VMEM((4, 2, 576), BF16),
            pltpu.VMEM((4, 128, 128), F32),
            pltpu.VMEM((4, 384, 128), F32),
            pltpu.VMEM((16, 128), F32),
            pltpu.VMEM((128, 640), F32),
            pltpu.VMEM((2, 16, 1152), BF16),
            pltpu.VMEM((2, 16, 128), BF16),
            pltpu.VMEM((2, 16, 128), BF16),
            pltpu.VMEM((2, 4, 16, 1152), BF16),
            pltpu.VMEM((2, 768, 640), BF16),
            pltpu.VMEM((2, 768, 512), BF16),
            pltpu.VMEM((2, 640, 768), BF16),
            pltpu.VMEM((2, 640, 768), BF16),
            pltpu.VMEM((2, 128, 640), BF16),
            pltpu.VMEM((2, 128, 640), BF16),
            pltpu.VMEM((2, 128, 512), BF16),
            pltpu.VMEM((2, 128, 128), F32),
            pltpu.VMEM((2, 4, 32, 640), BF16),
            pltpu.VMEM((2, 4, 32, 640), BF16),
            pltpu.VMEM((2, 4, 16, 1152), BF16),
            pltpu.VMEM((2, 4, 16, 1152), BF16),
            pltpu.VMEM((4, 32, 512), F32),
            pltpu.VMEM((4, 32, 128), F32),
            pltpu.VMEM((2, 32, 512), BF16),
            pltpu.VMEM((4, 32, 512), BF16),
            pltpu.SMEM((128,), jnp.int32),
            pltpu.SMEM((4,), jnp.int32),
            pltpu.SMEM((1, 2), jnp.int32),
            dma((32,)),
            dma((5,)),
            dma((5,)),
            dma((4, 4)),
            dma((4, 4)),
            dma((4,)),
            dma((4,)),
            dma((2,)),
            dma((2,)),
            dma((2, 4)),
            dma((2, 4)),
            dma((4, 4)),
            dma((4, 4)),
            dma((4,)),
            dma((4,)),
        ],
        compiler_params=pltpu.CompilerParams(
            collective_id=0, has_side_effects=True, vmem_limit_bytes=48 * 1024 * 1024
        ),
        cost_estimate=pl.CostEstimate(flops=1800000000, bytes_accessed=4800000, transcendentals=800000),
    )(
        *[
            pltpu.with_memory_space_constraint(x, pltpu.HBM)
            for x in (
                jnp.asarray(plan_table()),
                lengths,
                move_slots,
                cache_latent.reshape(4, 768, 512),
                cache_rope.transpose(1, 0, 2),
                q_latent,
                q_rope,
                new_keys,
            )
        ]
    )
    return out.reshape(4, 2, 16, 512)


def solution(mesh):
    in_specs = (
        P("rep", "ctx", None, None),
        P("rep", "ctx", None),
        P("rep"),
        P("rep", None),
        P("rep", None, None, None),
        P("rep", None, None),
        P("rep", None, None),
    )
    out_specs = P("rep", None, "ctx", None)
    return jax.shard_map(body, mesh=mesh, in_specs=in_specs, out_specs=out_specs, check_vma=False)
```
